32 devices in a mesh: seq: 8 (over z, x), exp: 4 (over y, core).
Axes of the slice: x: 2, y: 2, z: 4, core: 2. Of those that a mesh axis runs over, the one named last changes fastest.
Arguments:
- residual_in: bfloat16 [4, 2048, 2048], P('exp', 'seq'), may hold values from -6 to 6
- query_matrix: bfloat16 [4, 2048, 2048], P('exp', 'seq'), may hold values from -6 to 6
- key_vectors: bfloat16 [4, 2048, 2048], P('exp', 'seq'), may hold values from -6 to 6
- value_vectors: bfloat16 [4, 2048, 2048], P('exp', 'seq'), may hold values from -6 to 6
- head_gain: float32 [2048], replicated, may hold values from 0.5 to 1.5
- norm_gain: float32 [2048], replicated, may hold values from 0.5 to 1.5
- expert_ids: int32 [4, 2048, 4], P('exp', 'seq'), may hold values from 0 to 7, all different within a row; in each aligned block of 256 rows (0 to 255, 256 to 511, ..., all dimensions but the last counted through in order) at most 192 rows name the same one
- gate_probs: float32 [4, 2048, 4], P('exp', 'seq'), may hold values from 0.25 to 1
- w_gate: bfloat16 [8, 2048, 1408], P('exp'), may hold values from -0.125 to 0.125
- w_up: bfloat16 [8, 2048, 1408], P('exp'), may hold values from -0.125 to 0.125
- w_down: bfloat16 [8, 1408, 2048], P('exp'), may hold values from -0.15625 to 0.15625
Outputs:
- layer_out: bfloat16 [4, 2048, 2048], P('exp', 'seq')
The draws below stay inside these ranges and needn't reach their ends.
Inputs may be any that keep to these rules, and one draw needn't show every extreme that they name: `expert_ids`: the 4 experts of one position differ; among the 256 positions of one device, no expert is named by more than 192 routes.
All inputs are finite; a program needn't handle non-finite values.
Results may differ from the reference program's by a relative error of at most 0.013.
Values may be sent and summed in bfloat16 or wider, within the bound.
A program may use at most 128 MiB of HBM per device.

```python
import math
import jax
import jax.numpy as jnp
import numpy as np
from jax import lax

D = 2048
HEADS = 16
HD = 128
FF = 1408
TOP = 4
EXPERTS = 8
TOK_DEV = 256
LEN = 2048
SEQS = 4
CAP = 192


def steps_of(key, extent, shards, least, top_value):
    def one(dim, blocks):
        heights = jax.random.uniform(jax.random.fold_in(jax.random.fold_in(key, 6), dim), (blocks,), jnp.float32, least / len(shards), top_value / len(shards))
        return jnp.repeat(jnp.exp(heights), extent[dim] // blocks).reshape((-1,) + (1,) * (len(extent) - dim - 1))

    loudness = one(*shards[0])
    for cut in shards[1:]:
        loudness = loudness * one(*cut)
    return loudness


def routed_block(key, own, number, rows, amount, top, most, skew):
    ranking = jax.random.permutation(key, amount)
    packed, common = shares(amount, rows * top, most, skew, True), shares(amount, rows * top, most, skew, False)
    places = jnp.arange(amount)

    def named(sizes, offset_by):
        used = int((sizes > 0).sum())
        fixed = max(1, used // 4)
        shifted = fixed + (places - fixed + offset_by * (used - fixed)) % max(1, amount - fixed)
        return jnp.zeros((amount,), jnp.int32).at[ranking[jnp.where(places < fixed, places, shifted)]].set(jnp.asarray(sizes, jnp.int32))

    sizes = jnp.where(number % 4 == 0, named(packed, number // 4), named(common, number - number // 4 - 1))
    mixed = jax.random.permutation(jax.random.fold_in(own, 3), amount)
    source_of, taker = mixed[0:amount // 2 * 2:2], mixed[1:amount // 2 * 2:2]
    margin = jnp.minimum(sizes[source_of] - 1, most - sizes[taker]) // 2
    margin = jnp.where((source_of == ranking[0]) | (taker == ranking[0]) | (sizes[taker] == 0), 0, jnp.maximum(margin, 0))
    shifted = jax.random.randint(jax.random.fold_in(own, 4), (amount // 2,), 0, 1 << 20) % (margin + 1)
    sizes = sizes.at[source_of].add(-shifted).at[taker].add(shifted)
    members = jnp.searchsorted(jnp.cumsum(sizes), jnp.arange(rows * top), side="right").astype(jnp.int32)
    listing = members.reshape(top, rows).T
    listing = listing[jax.random.permutation(jax.random.fold_in(own, 1), rows)]
    offset_by = jax.random.randint(jax.random.fold_in(own, 2), (rows, 1), 0, top)
    return jnp.take_along_axis(listing, (jnp.arange(top)[None, :] + offset_by) % top, axis=1)


def shares(number_of, total, most, skew, full):
    weights = [(1 << 20) // math.isqrt(standing ** skew) + 1 for standing in range(1, number_of + 1)]
    largest = most if full else min(most, max(-(-total // number_of), total * weights[0] // sum(weights)))
    least = 1 if total - largest >= number_of - 1 else 0
    holding, surplus = [largest] + [least] * (number_of - 1), total - largest - least * (number_of - 1)
    while surplus > 0:
        free = [i for i in range(1, number_of) if holding[i] < largest] or [i for i in range(1, number_of) if holding[i] < most]
        whole, remaining = sum([weights[i] for i in free]), surplus
        for i in free:
            addition = min(most - holding[i], max(1, remaining * weights[i] // whole), surplus)
            holding[i] = holding[i] + addition
            surplus = surplus - addition
    return np.array(holding)


def scatter_about(rng, extent, width, bound, cuts=(), held_as=jnp.bfloat16):
    array = width * jax.random.normal(rng, extent, jnp.float32)
    if cuts:
        array = array * steps_of(rng, extent, cuts, -0.22, 0.18)
    return jnp.clip(array, -bound, bound).astype(held_as)


def setup_inputs(seed: int = 0) -> dict:
    splits = jax.random.split(jax.random.key(seed), 12)
    residual_in = scatter_about(splits[0], (SEQS, LEN, D), 1.0, 6.0, ((0, 4), (1, 8)))
    query_matrix = scatter_about(splits[1], (SEQS, LEN, D), 1.0, 6.0, ((0, 4), (1, 8)))
    key_vectors = scatter_about(splits[2], (SEQS, LEN, D), 1.0, 6.0, ((0, 4), (1, 8)))
    value_vectors = scatter_about(splits[3], (SEQS, LEN, D), 1.0, 6.0, ((0, 4), (1, 8)))
    head_gain = jnp.clip(1.0 + 0.1 * jax.random.normal(splits[4], (D,), jnp.float32), 0.5, 1.5)
    norm_gain = jnp.clip(1.0 + 0.1 * jax.random.normal(splits[5], (D,), jnp.float32), 0.5, 1.5)
    expert_ids_keys = jax.random.split(jax.random.fold_in(splits[6], 1), SEQS * LEN // TOK_DEV)
    expert_ids_turns = jax.random.permutation(jax.random.fold_in(splits[6], 3), SEQS * LEN // TOK_DEV)
    expert_ids = jax.vmap(lambda own, number: routed_block(jax.random.fold_in(splits[6], 2), own, number, TOK_DEV, EXPERTS, TOP, CAP, 2))(expert_ids_keys, expert_ids_turns).reshape((SEQS, LEN, TOP))
    gate_probs = jnp.clip(0.25 + 0.75 * jax.random.uniform(splits[7], (SEQS, LEN, TOP), jnp.float32) ** steps_of(splits[7], (SEQS, LEN, TOP), ((0, 4), (1, 8)), -0.2, 0.2), 0.25, 1.0)
    w_gate = scatter_about(splits[8], (EXPERTS, D, FF), D ** -0.5, 0.125, ((0, 4),))
    w_up = scatter_about(splits[9], (EXPERTS, D, FF), D ** -0.5, 0.125, ((0, 4),))
    w_down = scatter_about(splits[10], (EXPERTS, FF, D), FF ** -0.5, 0.15625, ((0, 4),))
    return {"residual_in": residual_in, "query_matrix": query_matrix, "key_vectors": key_vectors, "value_vectors": value_vectors, "head_gain": head_gain, "norm_gain": norm_gain, "expert_ids": expert_ids, "gate_probs": gate_probs, "w_gate": w_gate, "w_up": w_up, "w_down": w_down}


def reference(residual_in, query_matrix, key_vectors, value_vectors, head_gain, norm_gain, expert_ids, gate_probs, w_gate, w_up, w_down):
    nblocks = LEN // TOK_DEV

    def split_heads(arr):
        return arr.astype(jnp.float32).reshape(SEQS, nblocks, TOK_DEV, HEADS, HD)
    queries = split_heads(query_matrix)
    key_rows = split_heads(key_vectors)
    value_rows = split_heads(value_vectors)
    states = jnp.einsum('sbthd,sbthe->sbhde', key_rows, value_rows)
    running = jnp.cumsum(states, axis=1)
    prefix = jnp.concatenate([jnp.zeros_like(states[:, :1]), running[:, :-1]], axis=1)
    prefix = lax.optimization_barrier(prefix.astype(jnp.bfloat16)).astype(jnp.float32)
    causal = jnp.tril(jnp.ones((TOK_DEV, TOK_DEV), dtype=bool))

    def per_sequence(item_entries):
        query_row_block, key_row_block, value_row_block, partial_state = item_entries
        scores = jnp.einsum('bthd,buhd->bhtu', query_row_block, key_row_block)
        weights = jnp.where(causal[None, None], scores, 0.0).astype(jnp.bfloat16)
        weights = lax.optimization_barrier(weights).astype(jnp.float32)
        inner = jnp.einsum('bhtu,buhd->bthd', weights, value_row_block)
        outer_product = jnp.einsum('urpw,upwa->urpa', query_row_block, partial_state)
        return inner + outer_product
    mixed = lax.map(per_sequence, (queries, key_rows, value_rows, prefix))
    mean_square = lax.optimization_barrier(jnp.mean(mixed * mixed, axis=-1, keepdims=True))
    attn = (mixed * lax.rsqrt(mean_square + 1e-06)).reshape(SEQS, LEN, D) * head_gain
    resid_sum = (residual_in.astype(jnp.float32) + attn).astype(jnp.bfloat16)
    resid_float = resid_sum.astype(jnp.float32)
    row_square = lax.optimization_barrier(jnp.mean(resid_float * resid_float, axis=-1, keepdims=True))
    normed = (resid_float * lax.rsqrt(row_square + 1e-06) * norm_gain).astype(jnp.bfloat16)
    rows = SEQS * LEN
    blocks = rows // TOK_DEV
    route_ids = expert_ids.reshape(blocks, TOK_DEV * TOP).astype(jnp.int32)
    expert_indicator = (route_ids[:, :, None] == jnp.arange(EXPERTS, dtype=jnp.int32)[None, None, :]).astype(jnp.int32)
    slots = lax.optimization_barrier(jnp.sum((jnp.cumsum(expert_indicator, axis=1) - expert_indicator) * expert_indicator, axis=2)).astype(jnp.int32)
    position = (jnp.arange(blocks, dtype=jnp.int32)[:, None] * CAP + slots).reshape(-1)
    token_of = (jnp.arange(blocks, dtype=jnp.int32)[:, None] * TOK_DEV + jnp.arange(TOK_DEV * TOP, dtype=jnp.int32)[None, :] // TOP).reshape(-1)
    flat_ids = route_ids.reshape(-1)
    flat_gates = gate_probs.reshape(-1).astype(jnp.float32)
    padded = jnp.concatenate([normed.reshape(rows, D), jnp.zeros((1, D), jnp.bfloat16)], axis=0)

    def one_expert(total, item_entries):
        expert, gate_mat, up_mat, down_mat = item_entries
        target = jnp.where(flat_ids == expert, position, blocks * CAP).astype(jnp.int32)
        index = jnp.full((blocks * CAP,), rows, jnp.int32).at[target].set(token_of, mode='drop')
        weight = jnp.zeros((blocks * CAP,), jnp.float32).at[target].set(flat_gates, mode='drop')
        chosen = padded[index]
        gate_part = jnp.dot(chosen, gate_mat, preferred_element_type=jnp.float32)
        up_part = jnp.dot(chosen, up_mat, preferred_element_type=jnp.float32)
        hidden = (jax.nn.silu(gate_part) * up_part).astype(jnp.bfloat16)
        result = jnp.dot(hidden, down_mat, preferred_element_type=jnp.float32).astype(jnp.bfloat16)
        total = total.at[index].add(result.astype(jnp.float32) * weight[:, None], mode='drop')
        return (total, None)
    total, _ = lax.scan(one_expert, jnp.zeros((rows, D), jnp.float32), (jnp.arange(EXPERTS, dtype=jnp.int32), w_gate, w_up, w_down))
    return (resid_float + total.reshape(SEQS, LEN, D)).astype(jnp.bfloat16)
```

```python
import functools

import jax
import jax.numpy as jnp
from jax import lax
from jax.experimental import pallas as pl
from jax.experimental.pallas import tpu as pltpu
from jax.sharding import PartitionSpec as P

HEADS = 16
HD = 128
EXPERTS = 8
CH = 2
NCH = HEADS // CH
ROWCH = 2
TN = 512
FT = 256
MESH = pl.DeviceIdType.MESH
BF = jnp.bfloat16
F32 = jnp.float32


def dot(a, b):
    return jnp.dot(a, b, preferred_element_type=F32)


def kernel(
    cfg, res, q, k, v, hg, ng, ids, probs, wg, wu, wd, out,
    st, stb, xb, zb, zo, acc, rs, sq, gall, xall, wgv, wuv, wdv, hid, gc, to,
    lsb, lrb, rsb, rrb, rown, ysb, yrb,
    wsem, gs, gr, xs, xr, zs, zr, ys, yr, ss, sr, ls, lr, ps, pr, bs, br,
):
    n_seq, n_exp, X, L, T, D, FF = cfg
    Z = n_seq // X
    Y = n_exp // 2
    NT = D // TN
    me_s = lax.axis_index("seq")
    me_e = lax.axis_index("exp")
    z = me_s // X
    x = me_s % X
    y = me_e // 2
    c = me_e % 2
    sib = y * 2 + 1 - c

    barrier = pltpu.get_barrier_semaphore()
    for d in range(1, X):
        pl.semaphore_signal(
            barrier, inc=1, device_id={"seq": z * X + (x + d) % X}, device_id_type=MESH
        )
    for d in range(1, n_exp):
        pl.semaphore_signal(
            barrier, inc=1, device_id={"exp": (me_e + d) % n_exp}, device_id_type=MESH
        )

    @pl.when(z > 0)
    def _():
        pl.semaphore_signal(barrier, inc=1, device_id={"seq": me_s - X}, device_id_type=MESH)

    @pl.when(z < Z - 1)
    def _():
        pl.semaphore_signal(barrier, inc=1, device_id={"seq": me_s + X}, device_id_type=MESH)

    wcopies = []
    for l in range(L):
        wcopies.append(pltpu.make_async_copy(wg.at[l], wgv.at[l], wsem.at[3 * l]))
        wcopies.append(pltpu.make_async_copy(wu.at[l], wuv.at[l], wsem.at[3 * l + 1]))
    for l in range(L):
        wcopies.append(
            pltpu.make_async_copy(
                wd.at[pl.ds(l * FF, FF)], wdv.at[pl.ds(l * FF, FF)], wsem.at[3 * l + 2]
            )
        )
    for w in wcopies:
        w.start()

    lane = lax.broadcasted_iota(jnp.int32, (T, HD), 1)
    g = jnp.zeros((T, HD), F32)
    for t in range(ids.shape[1]):
        g = g + jnp.where(lane == ids[:, t : t + 1], probs[:, t : t + 1], 0.0)
    gall[me_e] = g.T[:EXPERTS]

    @pl.when(z == 0)
    def _():
        zb[...] = jnp.zeros_like(zb)

    pl.semaphore_wait(
        barrier,
        X - 1 + n_exp - 1 + jnp.where(z > 0, 1, 0) + jnp.where(z < Z - 1, 1, 0),
    )

    def remote(src, dst, send, recv, where):
        return pltpu.make_async_remote_copy(
            src_ref=src, dst_ref=dst, send_sem=send, recv_sem=recv,
            device_id=where, device_id_type=MESH,
        )

    def gcopy(d, owner):
        return remote(
            gall.at[owner], gall.at[owner], gs.at[d - 1], gr.at[d - 1],
            {"exp": (me_e + d) % n_exp},
        )

    def xcopy(d, i):
        sl = pl.ds(i * CH, CH)
        return remote(
            stb.at[sl], xb.at[d - 1, sl], xs.at[d - 1, i], xr.at[d - 1, i],
            {"seq": z * X + (x + d) % X},
        )

    def zcopy(i):
        sl = pl.ds(i * CH, CH)
        return remote(
            zo.at[sl], zb.at[sl], zs.at[i], zr.at[i],
            {"seq": jnp.minimum(me_s + X, n_seq - 1)},
        )

    for d in range(1, n_exp):
        gcopy(d, me_e).start()

    def cols_of(h):
        return pl.ds(pl.multiple_of(h * HD, HD), HD)

    def state_body(i, carry):
        for hh in range(CH):
            h = i * CH + hh
            cols = cols_of(h)
            s = lax.dot_general(
                k[:, cols], v[:, cols], (((0,), (0,)), ((), ())), preferred_element_type=F32
            )
            st[h] = s
            stb[h] = s.astype(BF)
        for d in range(1, X):
            xcopy(d, i).start()
        return carry

    lax.fori_loop(0, NCH, state_body, 0)

    sq[...] = jnp.zeros_like(sq)
    causal = lax.broadcasted_iota(jnp.int32, (T, T), 0) >= lax.broadcasted_iota(
        jnp.int32, (T, T), 1
    )

    def inner_body(i, carry):
        for hh in range(CH):
            cols = cols_of(i * CH + hh)
            s = lax.dot_general(
                q[:, cols], k[:, cols], (((1,), (1,)), ((), ())), preferred_element_type=F32
            )
            w = jnp.where(causal, s, 0.0).astype(BF)
            acc[:, cols] = dot(w, v[:, cols])
        return carry

    lax.fori_loop(0, NCH, inner_body, 0)

    def chain_body(i, carry):
        sl = pl.ds(i * CH, CH)
        t = st[sl]
        before = jnp.zeros_like(t)
        for d in range(1, X):
            xcopy(d, i).wait_recv()
            r = xb[d - 1, sl].astype(F32)
            t = t + r
            before = before + jnp.where(x >= d, r, 0.0)

        @pl.when(z > 0)
        def _():
            zcopy(i).wait_recv()

        p = zb[sl].astype(F32)

        @pl.when(z < Z - 1)
        def _():
            zo[sl] = (p + t).astype(BF)
            zcopy(i).start()

        pf = (p + before).astype(BF)
        for hh in range(CH):
            cols = cols_of(i * CH + hh)
            m = acc[:, cols] + dot(q[:, cols], pf[hh])
            ms = jnp.mean(m * m, axis=-1, keepdims=True)
            a = m * lax.rsqrt(ms + 1e-06) * hg[:, cols]
            r = (res[:, cols].astype(F32) + a).astype(BF)
            rs[:, cols] = r
            rf = r.astype(F32)
            sq[...] += rf * rf
        return carry

    lax.fori_loop(0, NCH, chain_body, 0)

    RC = T // ROWCH

    def block_rows(owner, r):
        return pl.ds(pl.multiple_of(owner * T + r * RC, RC), RC)

    def ycopy(dy, r, owner):
        rows = block_rows(owner, r)
        return remote(
            xall.at[rows], xall.at[rows], ys.at[dy - 1, r], yr.at[dy - 1, r],
            {"exp": ((y + dy) % Y) * 2 + c},
        )

    def scopy(dy, r, owner):
        rows = block_rows(owner, r)
        return remote(
            xall.at[rows], xall.at[rows], ss.at[dy, r], sr.at[dy, r], {"exp": sib}
        )

    for r in range(ROWCH):
        part = slice(r * RC, (r + 1) * RC)
        inv = lax.rsqrt(jnp.sum(sq[part], axis=-1, keepdims=True) / D + 1e-06)
        xall[block_rows(me_e, r)] = (rs[part].astype(F32) * inv * ng[...]).astype(BF)
        for dy in range(1, Y):
            ycopy(dy, r, me_e).start()
        scopy(0, r, me_e).start()

    def from_y(dy):
        return (y + Y - dy) % Y

    def gates(yy):
        for l in range(L):
            for b in range(2):
                gt = gall[yy * 2 + b].T
                pick = lax.broadcasted_iota(jnp.int32, (T, EXPERTS), 1) == me_e * L + l
                col = jnp.sum(jnp.where(pick, gt, 0.0), axis=1, keepdims=True)
                gc[l, b * T : (b + 1) * T] = jnp.broadcast_to(col, (T, HD))

    def act(gp, up, gate):
        return (0.5 * gp * (1.0 + jnp.tanh(0.5 * gp)) * up * gate).astype(BF)

    def gate_up(yy, first):
        rows = pl.ds(pl.multiple_of(yy * 2 * T, 2 * T), 2 * T)
        for l in range(L):
            if first:
                wcopies[2 * l].wait()
                wcopies[2 * l + 1].wait()

            def body(j, carry):
                cols = pl.ds(pl.multiple_of(j * FT, FT), FT)
                xv = xall[rows]
                gp = dot(xv, wgv[l, :, cols])
                up = dot(xv, wuv[l, :, cols])
                gate = jnp.concatenate([gc[l]] * (FT // HD), axis=1)
                hid[:, pl.ds(pl.multiple_of(l * FF + j * FT, HD), FT)] = act(gp, up, gate)
                return carry

            full = FF // FT
            lax.fori_loop(0, full, body, 0)
            tail = FF - full * FT
            if tail:
                w = jnp.concatenate([wgv[l, :, full * FT :], wuv[l, :, full * FT :]], axis=1)
                o = dot(xall[rows], w)
                gate = jnp.concatenate([gc[l]] * (tail // HD), axis=1)
                hid[:, l * FF + full * FT : (l + 1) * FF] = act(o[:, :tail], o[:, tail:], gate)

    own = pl.ds(pl.multiple_of(c * T, T), T)
    other = pl.ds(pl.multiple_of((1 - c) * T, T), T)

    def lcopy(j):
        return remote(lsb.at[j], lrb.at[j], ls.at[j], lr.at[j], {"exp": sib})

    def pcopy(dy, j):
        return remote(
            rsb.at[dy - 1, j], rrb.at[dy - 1, j], ps.at[dy - 1, j], pr.at[dy - 1, j],
            {"exp": sib},
        )

    def bcopy(dy, j):
        return remote(
            ysb.at[dy - 1, j], yrb.at[dy - 1, j], bs.at[dy - 1, j], br.at[dy - 1, j],
            {"exp": from_y(dy) * 2 + c},
        )

    def tile_of(j):
        return pl.ds(pl.multiple_of(j * TN, TN), TN)

    for d in range(1, n_exp):
        gcopy(d, (me_e + n_exp - d) % n_exp).wait_recv()
    gates(y)
    for r in range(ROWCH):
        scopy(0, r, sib).wait_recv()
    gate_up(y, True)

    def forward(dy, r):
        owner = from_y(dy) * 2 + c
        ycopy(dy, r, owner).wait_recv()
        scopy(dy, r, owner).start()

    for dy in range(1, Y):
        forward(dy, 0)
    for l in range(L):
        wcopies[2 * L + l].wait()

    def local_down(j, carry):
        cols = tile_of(j)
        to[...] = dot(hid[...], wdv[:, cols])
        lsb[j] = to[other].astype(BF)
        lcopy(j).start()
        acc[:, cols] = to[own] + rs[:, cols].astype(F32)
        return carry

    lax.fori_loop(0, NT, local_down, 0)

    for dy in range(1, Y):
        for r in range(1, ROWCH):
            forward(dy, r)
        gates(from_y(dy))
        for r in range(ROWCH):
            scopy(dy, r, from_y(dy) * 2 + 1 - c).wait_recv()
        gate_up(from_y(dy), False)

        def combine(j):
            pcopy(dy, j).wait_recv()
            ysb[dy - 1, j] = (rown[j % 2] + rrb[dy - 1, j].astype(F32)).astype(BF)
            bcopy(dy, j).start()

        def remote_down(j, carry):
            to[...] = dot(hid[...], wdv[:, tile_of(j)])
            rsb[dy - 1, j] = to[other].astype(BF)
            pcopy(dy, j).start()
            rown[j % 2] = to[own]

            @pl.when(j > 0)
            def _():
                combine(j - 1)

            return carry

        lax.fori_loop(0, NT, remote_down, 0)
        combine(NT - 1)

    def add_local(j, carry):
        lcopy(j).wait_recv()
        acc[:, tile_of(j)] += lrb[j].astype(F32)
        return carry

    lax.fori_loop(0, NT, add_local, 0)

    def final(j, carry):
        cols = tile_of(j)
        a = acc[:, cols]
        for dy in range(1, Y):
            bcopy(dy, j).wait_recv()
            a = a + yrb[dy - 1, j].astype(F32)
        out[:, cols] = a.astype(BF)
        return carry

    lax.fori_loop(0, NT, final, 0)

    for d in range(1, n_exp):
        gcopy(d, me_e).wait_send()

    def sent_states(i, carry):
        for d in range(1, X):
            xcopy(d, i).wait_send()

        @pl.when(z < Z - 1)
        def _():
            zcopy(i).wait_send()

        return carry

    lax.fori_loop(0, NCH, sent_states, 0)
    for r in range(ROWCH):
        scopy(0, r, me_e).wait_send()
        for dy in range(1, Y):
            ycopy(dy, r, me_e).wait_send()
            scopy(dy, r, from_y(dy) * 2 + c).wait_send()

    def sent_parts(j, carry):
        lcopy(j).wait_send()
        for dy in range(1, Y):
            pcopy(dy, j).wait_send()
            bcopy(dy, j).wait_send()
        return carry

    lax.fori_loop(0, NT, sent_parts, 0)


def on_device(
    n_seq, n_exp,
    residual_in, query_matrix, key_vectors, value_vectors, head_gain, norm_gain,
    expert_ids, gate_probs, w_gate, w_up, w_down,
):
    T, D = residual_in.shape[1:]
    L, _, FF = w_gate.shape
    X = max(1, n_seq // 4)
    Y = n_exp // 2
    NT = D // TN
    cfg = (n_seq, n_exp, X, L, T, D, FF)
    DMA = pltpu.SemaphoreType.DMA
    vm = pl.BlockSpec(memory_space=pltpu.VMEM)
    anyspace = pl.BlockSpec(memory_space=pl.ANY)
    V = pltpu.VMEM
    y1 = max(1, Y - 1)
    x1 = max(1, X - 1)
    out = pl.pallas_call(
        functools.partial(kernel, cfg),
        out_shape=jax.ShapeDtypeStruct((T, D), BF),
        in_specs=[vm] * 8 + [anyspace] * 3,
        out_specs=vm,
        scratch_shapes=[
            V((HEADS, HD, HD), F32),
            V((HEADS, HD, HD), BF),
            V((x1, HEADS, HD, HD), BF),
            V((HEADS, HD, HD), BF),
            V((HEADS, HD, HD), BF),
            V((T, D), F32),
            V((T, D), BF),
            V((T, HD), F32),
            V((n_exp, EXPERTS, T), F32),
            V((n_exp * T, D), BF),
            V((L, D, FF), BF),
            V((L, D, FF), BF),
            V((L * FF, D), BF),
            V((2 * T, L * FF), BF),
            V((L, 2 * T, HD), F32),
            V((2 * T, TN), F32),
            V((NT, T, TN), BF),
            V((NT, T, TN), BF),
            V((y1, NT, T, TN), BF),
            V((y1, NT, T, TN), BF),
            V((2, T, TN), F32),
            V((y1, NT, T, TN), BF),
            V((y1, NT, T, TN), BF),
            DMA((3 * L,)),
            DMA((n_exp - 1,)),
            DMA((n_exp - 1,)),
            DMA((x1, NCH)),
            DMA((x1, NCH)),
            DMA((NCH,)),
            DMA((NCH,)),
            DMA((y1, ROWCH)),
            DMA((y1, ROWCH)),
            DMA((Y, ROWCH)),
            DMA((Y, ROWCH)),
            DMA((NT,)),
            DMA((NT,)),
            DMA((y1, NT)),
            DMA((y1, NT)),
            DMA((y1, NT)),
            DMA((y1, NT)),
        ],
        compiler_params=pltpu.CompilerParams(
            collective_id=0, has_side_effects=True, vmem_limit_bytes=63 * 1024 * 1024
        ),
        cost_estimate=pl.CostEstimate(
            flops=2 * n_exp * T * L * D * FF * 3, bytes_accessed=6 * L * D * FF, transcendentals=0
        ),
    )(
        residual_in[0], query_matrix[0], key_vectors[0], value_vectors[0],
        head_gain[None], norm_gain[None], expert_ids[0], gate_probs[0],
        w_gate, w_up, w_down.reshape(L * FF, D),
    )
    return out[None]


def solution(mesh):
    rows = P("exp", "seq", None)
    experts = P("exp", None, None)
    in_specs = (rows, rows, rows, rows, P(), P(), rows, rows, experts, experts, experts)
    return jax.shard_map(
        functools.partial(on_device, mesh.shape["seq"], mesh.shape["exp"]),
        mesh=mesh, in_specs=in_specs, out_specs=rows, check_vma=False,
    )
```

```python
import functools

import jax
import jax.numpy as jnp
from jax import lax
from jax.experimental import pallas as pl
from jax.experimental.pallas import tpu as pltpu
from jax.sharding import PartitionSpec as P

HEADS = 16
HD = 128
EXPERTS = 8
CH = 2
NCH = HEADS // CH
ROWCH = 2
TN = 512
FT = 256
MESH = pl.DeviceIdType.MESH
BF = jnp.bfloat16
F32 = jnp.float32


def dot(a, b):
    return jnp.dot(a, b, preferred_element_type=F32)


def kernel(
    cfg, res, q, k, v, hg, ng, ids, probs, wg, wu, wd, out,
    st, stb, xb, zb, zo, acc, rs, sq, gall, xall, wgv, wuv, wdv, hid, gc, to,
    lsb, lrb, rsb, rrb, rown, ysb, yrb,
    wsem, gs, gr, xs, xr, zs, zr, ys, yr, ss, sr, ls, lr, ps, pr, bs, br,
):
    n_seq, n_exp, X, L, T, D, FF = cfg
    Z = n_seq // X
    Y = n_exp // 2
    NT = D // TN
    me_s = lax.axis_index("seq")
    me_e = lax.axis_index("exp")
    z = me_s // X
    x = me_s % X
    y = me_e // 2
    c = me_e % 2
    sib = y * 2 + 1 - c

    barrier = pltpu.get_barrier_semaphore()
    for d in range(1, X):
        pl.semaphore_signal(
            barrier, inc=1, device_id={"seq": z * X + (x + d) % X}, device_id_type=MESH
        )
    for d in range(1, n_exp):
        pl.semaphore_signal(
            barrier, inc=1, device_id={"exp": (me_e + d) % n_exp}, device_id_type=MESH
        )

    @pl.when(z > 0)
    def _():
        pl.semaphore_signal(barrier, inc=1, device_id={"seq": me_s - X}, device_id_type=MESH)

    @pl.when(z < Z - 1)
    def _():
        pl.semaphore_signal(barrier, inc=1, device_id={"seq": me_s + X}, device_id_type=MESH)

    wcopies = []
    for l in range(L):
        wcopies.append(pltpu.make_async_copy(wg.at[l], wgv.at[l], wsem.at[3 * l]))
        wcopies.append(pltpu.make_async_copy(wu.at[l], wuv.at[l], wsem.at[3 * l + 1]))
    for l in range(L):
        wcopies.append(
            pltpu.make_async_copy(
                wd.at[pl.ds(l * FF, FF)], wdv.at[pl.ds(l * FF, FF)], wsem.at[3 * l + 2]
            )
        )
    for w in wcopies:
        w.start()

    expert = lax.broadcasted_iota(jnp.int32, (EXPERTS, T), 0)
    g = jnp.zeros((EXPERTS, T), F32)
    for t in range(ids.shape[0]):
        g = g + jnp.where(expert == ids[t : t + 1], probs[t : t + 1], 0.0)
    gall[me_e] = g

    @pl.when(z == 0)
    def _():
        zb[...] = jnp.zeros_like(zb)

    pl.semaphore_wait(
        barrier,
        X - 1 + n_exp - 1 + jnp.where(z > 0, 1, 0) + jnp.where(z < Z - 1, 1, 0),
    )

    def remote(src, dst, send, recv, where):
        return pltpu.make_async_remote_copy(
            src_ref=src, dst_ref=dst, send_sem=send, recv_sem=recv,
            device_id=where, device_id_type=MESH,
        )

    def gcopy(d, owner):
        return remote(
            gall.at[owner], gall.at[owner], gs.at[d - 1], gr.at[d - 1],
            {"exp": (me_e + d) % n_exp},
        )

    def xcopy(d, i):
        sl = pl.ds(i * CH, CH)
        return remote(
            stb.at[sl], xb.at[d - 1, sl], xs.at[d - 1, i], xr.at[d - 1, i],
            {"seq": z * X + (x + d) % X},
        )

    def zcopy(i):
        sl = pl.ds(i * CH, CH)
        return remote(
            zo.at[sl], zb.at[sl], zs.at[i], zr.at[i],
            {"seq": jnp.minimum(me_s + X, n_seq - 1)},
        )

    for d in range(1, n_exp):
        gcopy(d, me_e).start()

    def cols_of(h):
        return pl.ds(pl.multiple_of(h * HD, HD), HD)

    def state_body(i, carry):
        for hh in range(CH):
            h = i * CH + hh
            cols = cols_of(h)
            s = lax.dot_general(
                k[:, cols], v[:, cols], (((0,), (0,)), ((), ())), preferred_element_type=F32
            )
            st[h] = s
            stb[h] = s.astype(BF)
        for d in range(1, X):
            xcopy(d, i).start()
        return carry

    lax.fori_loop(0, NCH, state_body, 0)

    sq[...] = jnp.zeros_like(sq)
    causal = lax.broadcasted_iota(jnp.int32, (T, T), 0) >= lax.broadcasted_iota(
        jnp.int32, (T, T), 1
    )

    def inner_body(i, carry):
        for hh in range(CH):
            cols = cols_of(i * CH + hh)
            s = lax.dot_general(
                q[:, cols], k[:, cols], (((1,), (1,)), ((), ())), preferred_element_type=F32
            )
            w = jnp.where(causal, s, 0.0).astype(BF)
            acc[:, cols] = dot(w, v[:, cols])
        return carry

    lax.fori_loop(0, NCH, inner_body, 0)

    def chain_body(i, carry):
        sl = pl.ds(i * CH, CH)
        t = st[sl]
        before = jnp.zeros_like(t)
        for d in range(1, X):
            xcopy(d, i).wait_recv()
            r = xb[d - 1, sl].astype(F32)
            t = t + r
            before = before + jnp.where(x >= d, r, 0.0)

        @pl.when(z > 0)
        def _():
            zcopy(i).wait_recv()

        p = zb[sl].astype(F32)

        @pl.when(z < Z - 1)
        def _():
            zo[sl] = (p + t).astype(BF)
            zcopy(i).start()

        pf = (p + before).astype(BF)
        for hh in range(CH):
            cols = cols_of(i * CH + hh)
            m = acc[:, cols] + dot(q[:, cols], pf[hh])
            ms = jnp.mean(m * m, axis=-1, keepdims=True)
            a = m * lax.rsqrt(ms + 1e-06) * hg[:, cols]
            r = (res[:, cols].astype(F32) + a).astype(BF)
            rs[:, cols] = r
            rf = r.astype(F32)
            sq[...] += rf * rf
        return carry

    lax.fori_loop(0, NCH, chain_body, 0)

    RC = T // ROWCH

    def block_rows(owner, r):
        return pl.ds(pl.multiple_of(((owner // 2 * ROWCH + r) * 2 + owner % 2) * RC, RC), RC)

    def ycopy(dy, r, owner):
        rows = block_rows(owner, r)
        return remote(
            xall.at[rows], xall.at[rows], ys.at[dy - 1, r], yr.at[dy - 1, r],
            {"exp": ((y + dy) % Y) * 2 + c},
        )

    def scopy(dy, r, owner):
        rows = block_rows(owner, r)
        return remote(
            xall.at[rows], xall.at[rows], ss.at[dy, r], sr.at[dy, r], {"exp": sib}
        )

    for r in range(ROWCH):
        part = slice(r * RC, (r + 1) * RC)
        inv = lax.rsqrt(jnp.sum(sq[part], axis=-1, keepdims=True) / D + 1e-06)
        xall[block_rows(me_e, r)] = (rs[part].astype(F32) * inv * ng[...]).astype(BF)
        for dy in range(1, Y):
            ycopy(dy, r, me_e).start()
        scopy(0, r, me_e).start()

    def from_y(dy):
        return (y + Y - dy) % Y

    def gates(yy):
        for l in range(L):
            for b in range(2):
                gt = gall[yy * 2 + b].T
                pick = lax.broadcasted_iota(jnp.int32, (T, EXPERTS), 1) == me_e * L + l
                col = jnp.sum(jnp.where(pick, gt, 0.0), axis=1, keepdims=True)
                for r in range(ROWCH):
                    at = (r * 2 + b) * RC
                    gc[l, at : at + RC] = jnp.broadcast_to(col[r * RC : (r + 1) * RC], (RC, HD))

    def act(gp, up, gate):
        return (0.5 * gp * (1.0 + jnp.tanh(0.5 * gp)) * up * gate).astype(BF)

    def gate_up(yy, r0, count, first):
        M = count * 2 * RC
        rows = pl.ds(pl.multiple_of((yy * ROWCH + r0) * 2 * RC, 2 * RC), M)
        grows = slice(r0 * 2 * RC, r0 * 2 * RC + M)
        for l in range(L):
            if first:
                wcopies[2 * l].wait()
                wcopies[2 * l + 1].wait()

            def body(j, carry):
                cols = pl.ds(pl.multiple_of(j * FT, FT), FT)
                xv = xall[rows]
                gp = dot(xv, wgv[l, :, cols])
                up = dot(xv, wuv[l, :, cols])
                gate = jnp.concatenate([gc[l, grows]] * (FT // HD), axis=1)
                hid[:M, pl.ds(pl.multiple_of(l * FF + j * FT, HD), FT)] = act(gp, up, gate)
                return carry

            full = FF // FT
            lax.fori_loop(0, full, body, 0)
            tail = FF - full * FT
            if tail:
                w = jnp.concatenate([wgv[l, :, full * FT :], wuv[l, :, full * FT :]], axis=1)
                o = dot(xall[rows], w)
                gate = jnp.concatenate([gc[l, grows]] * (tail // HD), axis=1)
                hid[:M, l * FF + full * FT : (l + 1) * FF] = act(o[:, :tail], o[:, tail:], gate)

    def half(r, core):
        return pl.ds(pl.multiple_of((r * 2 + core) * RC, RC), RC)

    def lcopy(j):
        return remote(lsb.at[j], lrb.at[j], ls.at[j], lr.at[j], {"exp": sib})

    def pcopy(dy, j):
        return remote(
            rsb.at[dy - 1, j], rrb.at[dy - 1, j], ps.at[dy - 1, j], pr.at[dy - 1, j],
            {"exp": sib},
        )

    def bcopy(dy, j):
        return remote(
            ysb.at[dy - 1, j], yrb.at[dy - 1, j], bs.at[dy - 1, j], br.at[dy - 1, j],
            {"exp": from_y(dy) * 2 + c},
        )

    def tile_of(j):
        return pl.ds(pl.multiple_of(j * TN, TN), TN)

    for d in range(1, n_exp):
        gcopy(d, (me_e + n_exp - d) % n_exp).wait_recv()
    gates(y)
    for r in range(ROWCH):
        scopy(0, r, sib).wait_recv()
    gate_up(y, 0, ROWCH, True)

    def forward(dy, r):
        owner = from_y(dy) * 2 + c
        ycopy(dy, r, owner).wait_recv()
        scopy(dy, r, owner).start()

    for dy in range(1, Y):
        forward(dy, 0)
    for l in range(L):
        wcopies[2 * L + l].wait()

    def local_down(j, carry):
        cols = tile_of(j)
        to[...] = dot(hid[...], wdv[:, cols])
        for r in range(ROWCH):
            lsb[j, r * RC : (r + 1) * RC] = to[half(r, 1 - c)].astype(BF)
        lcopy(j).start()
        for r in range(ROWCH):
            part = slice(r * RC, (r + 1) * RC)
            acc[part, cols] = to[half(r, c)] + rs[part, cols].astype(F32)
        return carry

    lax.fori_loop(0, NT, local_down, 0)

    for dy in range(1, Y):
        gates(from_y(dy))
        for r in range(ROWCH):
            scopy(dy, r, from_y(dy) * 2 + 1 - c).wait_recv()
            gate_up(from_y(dy), r, 1, False)
            if r + 1 < ROWCH:
                forward(dy, r + 1)

            def combine(j, i):
                pcopy(dy, i).wait_recv()
                ysb[dy - 1, i] = (rown[j % 2] + rrb[dy - 1, i].astype(F32)).astype(BF)
                bcopy(dy, i).start()

            def remote_down(j, carry):
                i = r * NT + j
                to[: 2 * RC] = dot(hid[: 2 * RC], wdv[:, tile_of(j)])
                rsb[dy - 1, i] = to[half(0, 1 - c)].astype(BF)
                pcopy(dy, i).start()
                rown[j % 2] = to[half(0, c)]

                @pl.when(j > 0)
                def _():
                    combine(j - 1, i - 1)

                return carry

            lax.fori_loop(0, NT, remote_down, 0)
            combine(NT - 1, r * NT + NT - 1)

    def add_local(j, carry):
        lcopy(j).wait_recv()
        acc[:, tile_of(j)] += lrb[j].astype(F32)
        return carry

    lax.fori_loop(0, NT, add_local, 0)

    def final(j, carry):
        cols = tile_of(j % NT)
        part = pl.ds(pl.multiple_of(j // NT * RC, RC), RC)
        a = acc[part, cols]
        for dy in range(1, Y):
            bcopy(dy, j).wait_recv()
            a = a + yrb[dy - 1, j].astype(F32)
        out[part, cols] = a.astype(BF)
        return carry

    lax.fori_loop(0, ROWCH * NT, final, 0)

    for d in range(1, n_exp):
        gcopy(d, me_e).wait_send()

    def sent_states(i, carry):
        for d in range(1, X):
            xcopy(d, i).wait_send()

        @pl.when(z < Z - 1)
        def _():
            zcopy(i).wait_send()

        return carry

    lax.fori_loop(0, NCH, sent_states, 0)
    for r in range(ROWCH):
        scopy(0, r, me_e).wait_send()
        for dy in range(1, Y):
            ycopy(dy, r, me_e).wait_send()
            scopy(dy, r, from_y(dy) * 2 + c).wait_send()

    def sent_parts(j, carry):
        for dy in range(1, Y):
            pcopy(dy, j).wait_send()
            bcopy(dy, j).wait_send()
        return carry

    lax.fori_loop(0, ROWCH * NT, sent_parts, 0)
    for j in range(NT):
        lcopy(j).wait_send()


def on_device(
    n_seq, n_exp,
    residual_in, query_matrix, key_vectors, value_vectors, head_gain, norm_gain,
    expert_ids, gate_probs, w_gate, w_up, w_down,
):
    T, D = residual_in.shape[1:]
    L, _, FF = w_gate.shape
    X = max(1, n_seq // 4)
    Y = n_exp // 2
    NT = D // TN
    cfg = (n_seq, n_exp, X, L, T, D, FF)
    DMA = pltpu.SemaphoreType.DMA
    vm = pl.BlockSpec(memory_space=pltpu.VMEM)
    anyspace = pl.BlockSpec(memory_space=pl.ANY)
    V = pltpu.VMEM
    y1 = max(1, Y - 1)
    x1 = max(1, X - 1)
    out = pl.pallas_call(
        functools.partial(kernel, cfg),
        out_shape=jax.ShapeDtypeStruct((T, D), BF),
        in_specs=[vm] * 8 + [anyspace] * 3,
        out_specs=vm,
        scratch_shapes=[
            V((HEADS, HD, HD), F32),
            V((HEADS, HD, HD), BF),
            V((x1, HEADS, HD, HD), BF),
            V((HEADS, HD, HD), BF),
            V((HEADS, HD, HD), BF),
            V((T, D), F32),
            V((T, D), BF),
            V((T, HD), F32),
            V((n_exp, EXPERTS, T), F32),
            V((n_exp * T, D), BF),
            V((L, D, FF), BF),
            V((L, D, FF), BF),
            V((L * FF, D), BF),
            V((2 * T, L * FF), BF),
            V((L, 2 * T, HD), F32),
            V((2 * T, TN), F32),
            V((NT, T, TN), BF),
            V((NT, T, TN), BF),
            V((y1, ROWCH * NT, T // ROWCH, TN), BF),
            V((y1, ROWCH * NT, T // ROWCH, TN), BF),
            V((2, T // ROWCH, TN), F32),
            V((y1, ROWCH * NT, T // ROWCH, TN), BF),
            V((y1, ROWCH * NT, T // ROWCH, TN), BF),
            DMA((3 * L,)),
            DMA((n_exp - 1,)),
            DMA((n_exp - 1,)),
            DMA((x1, NCH)),
            DMA((x1, NCH)),
            DMA((NCH,)),
            DMA((NCH,)),
            DMA((y1, ROWCH)),
            DMA((y1, ROWCH)),
            DMA((Y, ROWCH)),
            DMA((Y, ROWCH)),
            DMA((NT,)),
            DMA((NT,)),
            DMA((y1, ROWCH * NT)),
            DMA((y1, ROWCH * NT)),
            DMA((y1, ROWCH * NT)),
            DMA((y1, ROWCH * NT)),
        ],
        compiler_params=pltpu.CompilerParams(
            collective_id=0, has_side_effects=True, vmem_limit_bytes=63 * 1024 * 1024
        ),
        cost_estimate=pl.CostEstimate(
            flops=2 * n_exp * T * L * D * FF * 3, bytes_accessed=6 * L * D * FF, transcendentals=0
        ),
    )(
        residual_in[0], query_matrix[0], key_vectors[0], value_vectors[0],
        head_gain[None], norm_gain[None], expert_ids[0].T, gate_probs[0].T,
        w_gate, w_up, w_down.reshape(L * FF, D),
    )
    return out[None]


def solution(mesh):
    rows = P("exp", "seq", None)
    experts = P("exp", None, None)
    in_specs = (rows, rows, rows, rows, P(), P(), rows, rows, experts, experts, experts)
    return jax.shard_map(
        functools.partial(on_device, mesh.shape["seq"], mesh.shape["exp"]),
        mesh=mesh, in_specs=in_specs, out_specs=rows, check_vma=False,
    )
```

```python
import functools

import jax
import jax.numpy as jnp
from jax import lax
from jax.experimental import pallas as pl
from jax.experimental.pallas import tpu as pltpu
from jax.sharding import PartitionSpec as P

HEADS = 16
HD = 128
EXPERTS = 8
CH = 2
NCH = HEADS // CH
ROWCH = 2
TN = 512
FT = 256
MESH = pl.DeviceIdType.MESH
BF = jnp.bfloat16
F32 = jnp.float32


def dot(a, b):
    return jnp.dot(a, b, preferred_element_type=F32)


def kernel(
    cfg, res, q, k, v, hg, ng, ids, probs, wg, wu, wd, out,
    st, stb, xb, zb, zo, acc, rs, sq, gall, xall, wgv, wuv, wdv, hid, gc, to,
    lsb, lrb, rsb, rrb, rown, ysb, yrb,
    wsem, gs, gr, xs, xr, zs, zr, ys, yr, ss, sr, ls, lr, ps, pr, bs, br,
):
    n_seq, n_exp, X, L, T, D, FF = cfg
    Z = n_seq // X
    Y = n_exp // 2
    NT = D // TN
    me_s = lax.axis_index("seq")
    me_e = lax.axis_index("exp")
    z = me_s // X
    x = me_s % X
    y = me_e // 2
    c = me_e % 2
    sib = y * 2 + 1 - c

    barrier = pltpu.get_barrier_semaphore()
    for d in range(1, X):
        pl.semaphore_signal(
            barrier, inc=1, device_id={"seq": z * X + (x + d) % X}, device_id_type=MESH
        )
    for d in range(1, n_exp):
        pl.semaphore_signal(
            barrier, inc=1, device_id={"exp": (me_e + d) % n_exp}, device_id_type=MESH
        )

    @pl.when(z > 0)
    def _():
        pl.semaphore_signal(barrier, inc=1, device_id={"seq": me_s - X}, device_id_type=MESH)

    @pl.when(z < Z - 1)
    def _():
        pl.semaphore_signal(barrier, inc=1, device_id={"seq": me_s + X}, device_id_type=MESH)

    wcopies = []
    for l in range(L):
        wcopies.append(pltpu.make_async_copy(wg.at[l], wgv.at[l], wsem.at[3 * l]))
        wcopies.append(pltpu.make_async_copy(wu.at[l], wuv.at[l], wsem.at[3 * l + 1]))
    for l in range(L):
        wcopies.append(
            pltpu.make_async_copy(
                wd.at[pl.ds(l * FF, FF)], wdv.at[pl.ds(l * FF, FF)], wsem.at[3 * l + 2]
            )
        )
    for w in wcopies:
        w.start()

    expert = lax.broadcasted_iota(jnp.int32, (EXPERTS, T), 0)
    g = jnp.zeros((EXPERTS, T), F32)
    for t in range(ids.shape[0]):
        g = g + jnp.where(expert == ids[t : t + 1], probs[t : t + 1], 0.0)
    gall[me_e] = g

    @pl.when(z == 0)
    def _():
        zb[...] = jnp.zeros_like(zb)

    pl.semaphore_wait(
        barrier,
        X - 1 + n_exp - 1 + jnp.where(z > 0, 1, 0) + jnp.where(z < Z - 1, 1, 0),
    )

    def remote(src, dst, send, recv, where):
        return pltpu.make_async_remote_copy(
            src_ref=src, dst_ref=dst, send_sem=send, recv_sem=recv,
            device_id=where, device_id_type=MESH,
        )

    def gcopy(d, owner):
        return remote(
            gall.at[owner], gall.at[owner], gs.at[d - 1], gr.at[d - 1],
            {"exp": (me_e + d) % n_exp},
        )

    def xcopy(d, i):
        sl = pl.ds(i * CH, CH)
        return remote(
            stb.at[sl], xb.at[d - 1, sl], xs.at[d - 1, i], xr.at[d - 1, i],
            {"seq": z * X + (x + d) % X},
        )

    def zcopy(i):
        sl = pl.ds(i * CH, CH)
        return remote(
            zo.at[sl], zb.at[sl], zs.at[i], zr.at[i],
            {"seq": jnp.minimum(me_s + X, n_seq - 1)},
        )

    for d in range(1, n_exp):
        gcopy(d, me_e).start()

    def cols_of(h):
        return pl.ds(pl.multiple_of(h * HD, HD), HD)

    def state_body(i, carry):
        for hh in range(CH):
            h = i * CH + hh
            cols = cols_of(h)
            s = lax.dot_general(
                k[:, cols], v[:, cols], (((0,), (0,)), ((), ())), preferred_element_type=F32
            )
            st[h] = s
            stb[h] = s.astype(BF)
        for d in range(1, X):
            xcopy(d, i).start()
        return carry

    lax.fori_loop(0, NCH, state_body, 0)

    sq[...] = jnp.zeros_like(sq)
    causal = lax.broadcasted_iota(jnp.int32, (T, T), 0) >= lax.broadcasted_iota(
        jnp.int32, (T, T), 1
    )

    def inner_body(i, carry):
        for hh in range(CH):
            cols = cols_of(i * CH + hh)
            s = lax.dot_general(
                q[:, cols], k[:, cols], (((1,), (1,)), ((), ())), preferred_element_type=F32
            )
            w = jnp.where(causal, s, 0.0).astype(BF)
            acc[:, cols] = dot(w, v[:, cols])
        return carry

    @pl.when(z > 0)
    def _():
        lax.fori_loop(0, NCH, inner_body, 0)

    def chain_body(i, carry):
        sl = pl.ds(i * CH, CH)
        t = st[sl]
        before = jnp.zeros_like(t)
        for d in range(1, X):
            xcopy(d, i).wait_recv()
            r = xb[d - 1, sl].astype(F32)
            t = t + r
            before = before + jnp.where(x >= d, r, 0.0)

        @pl.when(z > 0)
        def _():
            zcopy(i).wait_recv()

        p = zb[sl].astype(F32)

        @pl.when(z < Z - 1)
        def _():
            zo[sl] = (p + t).astype(BF)
            zcopy(i).start()

        @pl.when(z == 0)
        def _():
            inner_body(i, 0)

        pf = (p + before).astype(BF)
        for hh in range(CH):
            cols = cols_of(i * CH + hh)
            m = acc[:, cols] + dot(q[:, cols], pf[hh])
            ms = jnp.mean(m * m, axis=-1, keepdims=True)
            a = m * lax.rsqrt(ms + 1e-06) * hg[:, cols]
            r = (res[:, cols].astype(F32) + a).astype(BF)
            rs[:, cols] = r
            rf = r.astype(F32)
            sq[...] += rf * rf
        return carry

    lax.fori_loop(0, NCH, chain_body, 0)

    RC = T // ROWCH

    def block_rows(owner, r):
        return pl.ds(pl.multiple_of(((owner // 2 * ROWCH + r) * 2 + owner % 2) * RC, RC), RC)

    def ycopy(dy, r, owner):
        rows = block_rows(owner, r)
        return remote(
            xall.at[rows], xall.at[rows], ys.at[dy - 1, r], yr.at[dy - 1, r],
            {"exp": ((y + dy) % Y) * 2 + c},
        )

    def scopy(dy, r, owner):
        rows = block_rows(owner, r)
        return remote(
            xall.at[rows], xall.at[rows], ss.at[dy, r], sr.at[dy, r], {"exp": sib}
        )

    for r in range(ROWCH):
        part = slice(r * RC, (r + 1) * RC)
        inv = lax.rsqrt(jnp.sum(sq[part], axis=-1, keepdims=True) / D + 1e-06)
        xall[block_rows(me_e, r)] = (rs[part].astype(F32) * inv * ng[...]).astype(BF)
        for dy in range(1, Y):
            ycopy(dy, r, me_e).start()
        scopy(0, r, me_e).start()

    def from_y(dy):
        return (y + Y - dy) % Y

    def gates(yy):
        for l in range(L):
            for b in range(2):
                gt = gall[yy * 2 + b].T
                pick = lax.broadcasted_iota(jnp.int32, (T, EXPERTS), 1) == me_e * L + l
                col = jnp.sum(jnp.where(pick, gt, 0.0), axis=1, keepdims=True)
                for r in range(ROWCH):
                    at = (r * 2 + b) * RC
                    gc[l, at : at + RC] = jnp.broadcast_to(col[r * RC : (r + 1) * RC], (RC, HD))

    def act(gp, up, gate):
        return (0.5 * gp * (1.0 + jnp.tanh(0.5 * gp)) * up * gate).astype(BF)

    def gate_up(yy, r0, count, first):
        M = count * 2 * RC
        rows = pl.ds(pl.multiple_of((yy * ROWCH + r0) * 2 * RC, 2 * RC), M)
        grows = slice(r0 * 2 * RC, r0 * 2 * RC + M)
        for l in range(L):
            if first:
                wcopies[2 * l].wait()
                wcopies[2 * l + 1].wait()

            def body(j, carry):
                cols = pl.ds(pl.multiple_of(j * FT, FT), FT)
                xv = xall[rows]
                gp = dot(xv, wgv[l, :, cols])
                up = dot(xv, wuv[l, :, cols])
                gate = jnp.concatenate([gc[l, grows]] * (FT // HD), axis=1)
                hid[:M, pl.ds(pl.multiple_of(l * FF + j * FT, HD), FT)] = act(gp, up, gate)
                return carry

            full = FF // FT
            lax.fori_loop(0, full, body, 0)
            tail = FF - full * FT
            if tail:
                w = jnp.concatenate([wgv[l, :, full * FT :], wuv[l, :, full * FT :]], axis=1)
                o = dot(xall[rows], w)
                gate = jnp.concatenate([gc[l, grows]] * (tail // HD), axis=1)
                hid[:M, l * FF + full * FT : (l + 1) * FF] = act(o[:, :tail], o[:, tail:], gate)

    def half(r, core):
        return pl.ds(pl.multiple_of((r * 2 + core) * RC, RC), RC)

    def lcopy(j):
        return remote(lsb.at[j], lrb.at[j], ls.at[j], lr.at[j], {"exp": sib})

    def pcopy(dy, j):
        return remote(
            rsb.at[dy - 1, j], rrb.at[dy - 1, j], ps.at[dy - 1, j], pr.at[dy - 1, j],
            {"exp": sib},
        )

    def bcopy(dy, j):
        return remote(
            ysb.at[dy - 1, j], yrb.at[dy - 1, j], bs.at[dy - 1, j], br.at[dy - 1, j],
            {"exp": from_y(dy) * 2 + c},
        )

    def tile_of(j):
        return pl.ds(pl.multiple_of(j * TN, TN), TN)

    for d in range(1, n_exp):
        gcopy(d, (me_e + n_exp - d) % n_exp).wait_recv()
    gates(y)
    for r in range(ROWCH):
        scopy(0, r, sib).wait_recv()
    gate_up(y, 0, ROWCH, True)

    def forward(dy, r):
        owner = from_y(dy) * 2 + c
        ycopy(dy, r, owner).wait_recv()
        scopy(dy, r, owner).start()

    for dy in range(1, Y):
        forward(dy, 0)
    for l in range(L):
        wcopies[2 * L + l].wait()

    def local_down(j, carry):
        cols = tile_of(j)
        to[...] = dot(hid[...], wdv[:, cols])
        for r in range(ROWCH):
            lsb[j, r * RC : (r + 1) * RC] = to[half(r, 1 - c)].astype(BF)
        lcopy(j).start()
        for r in range(ROWCH):
            part = slice(r * RC, (r + 1) * RC)
            acc[part, cols] = to[half(r, c)] + rs[part, cols].astype(F32)
        return carry

    lax.fori_loop(0, NT, local_down, 0)

    for dy in range(1, Y):
        gates(from_y(dy))
        for r in range(ROWCH):
            scopy(dy, r, from_y(dy) * 2 + 1 - c).wait_recv()
            gate_up(from_y(dy), r, 1, False)
            if r + 1 < ROWCH:
                forward(dy, r + 1)

            def combine(j, i):
                pcopy(dy, i).wait_recv()
                ysb[dy - 1, i] = (rown[j % 2] + rrb[dy - 1, i].astype(F32)).astype(BF)
                bcopy(dy, i).start()

            def remote_down(j, carry):
                i = r * NT + j
                to[: 2 * RC] = dot(hid[: 2 * RC], wdv[:, tile_of(j)])
                rsb[dy - 1, i] = to[half(0, 1 - c)].astype(BF)
                pcopy(dy, i).start()
                rown[j % 2] = to[half(0, c)]

                @pl.when(j > 0)
                def _():
                    combine(j - 1, i - 1)

                return carry

            lax.fori_loop(0, NT, remote_down, 0)
            combine(NT - 1, r * NT + NT - 1)

    def add_local(j, carry):
        lcopy(j).wait_recv()
        acc[:, tile_of(j)] += lrb[j].astype(F32)
        return carry

    lax.fori_loop(0, NT, add_local, 0)

    def final(j, carry):
        cols = tile_of(j % NT)
        part = pl.ds(pl.multiple_of(j // NT * RC, RC), RC)
        a = acc[part, cols]
        for dy in range(1, Y):
            bcopy(dy, j).wait_recv()
            a = a + yrb[dy - 1, j].astype(F32)
        out[part, cols] = a.astype(BF)
        return carry

    lax.fori_loop(0, ROWCH * NT, final, 0)

    for d in range(1, n_exp):
        gcopy(d, me_e).wait_send()

    def sent_states(i, carry):
        for d in range(1, X):
            xcopy(d, i).wait_send()

        @pl.when(z < Z - 1)
        def _():
            zcopy(i).wait_send()

        return carry

    lax.fori_loop(0, NCH, sent_states, 0)
    for r in range(ROWCH):
        scopy(0, r, me_e).wait_send()
        for dy in range(1, Y):
            ycopy(dy, r, me_e).wait_send()
            scopy(dy, r, from_y(dy) * 2 + c).wait_send()

    def sent_parts(j, carry):
        for dy in range(1, Y):
            pcopy(dy, j).wait_send()
            bcopy(dy, j).wait_send()
        return carry

    lax.fori_loop(0, ROWCH * NT, sent_parts, 0)
    for j in range(NT):
        lcopy(j).wait_send()


def on_device(
    n_seq, n_exp,
    residual_in, query_matrix, key_vectors, value_vectors, head_gain, norm_gain,
    expert_ids, gate_probs, w_gate, w_up, w_down,
):
    T, D = residual_in.shape[1:]
    L, _, FF = w_gate.shape
    X = max(1, n_seq // 4)
    Y = n_exp // 2
    NT = D // TN
    cfg = (n_seq, n_exp, X, L, T, D, FF)
    DMA = pltpu.SemaphoreType.DMA
    vm = pl.BlockSpec(memory_space=pltpu.VMEM)
    anyspace = pl.BlockSpec(memory_space=pl.ANY)
    V = pltpu.VMEM
    y1 = max(1, Y - 1)
    x1 = max(1, X - 1)
    out = pl.pallas_call(
        functools.partial(kernel, cfg),
        out_shape=jax.ShapeDtypeStruct((T, D), BF),
        in_specs=[vm] * 8 + [anyspace] * 3,
        out_specs=vm,
        scratch_shapes=[
            V((HEADS, HD, HD), F32),
            V((HEADS, HD, HD), BF),
            V((x1, HEADS, HD, HD), BF),
            V((HEADS, HD, HD), BF),
            V((HEADS, HD, HD), BF),
            V((T, D), F32),
            V((T, D), BF),
            V((T, HD), F32),
            V((n_exp, EXPERTS, T), F32),
            V((n_exp * T, D), BF),
            V((L, D, FF), BF),
            V((L, D, FF), BF),
            V((L * FF, D), BF),
            V((2 * T, L * FF), BF),
            V((L, 2 * T, HD), F32),
            V((2 * T, TN), F32),
            V((NT, T, TN), BF),
            V((NT, T, TN), BF),
            V((y1, ROWCH * NT, T // ROWCH, TN), BF),
            V((y1, ROWCH * NT, T // ROWCH, TN), BF),
            V((2, T // ROWCH, TN), F32),
            V((y1, ROWCH * NT, T // ROWCH, TN), BF),
            V((y1, ROWCH * NT, T // ROWCH, TN), BF),
            DMA((3 * L,)),
            DMA((n_exp - 1,)),
            DMA((n_exp - 1,)),
            DMA((x1, NCH)),
            DMA((x1, NCH)),
            DMA((NCH,)),
            DMA((NCH,)),
            DMA((y1, ROWCH)),
            DMA((y1, ROWCH)),
            DMA((Y, ROWCH)),
            DMA((Y, ROWCH)),
            DMA((NT,)),
            DMA((NT,)),
            DMA((y1, ROWCH * NT)),
            DMA((y1, ROWCH * NT)),
            DMA((y1, ROWCH * NT)),
            DMA((y1, ROWCH * NT)),
        ],
        compiler_params=pltpu.CompilerParams(
            collective_id=0, has_side_effects=True, vmem_limit_bytes=63 * 1024 * 1024
        ),
        cost_estimate=pl.CostEstimate(
            flops=2 * n_exp * T * L * D * FF * 3, bytes_accessed=6 * L * D * FF, transcendentals=0
        ),
    )(
        residual_in[0], query_matrix[0], key_vectors[0], value_vectors[0],
        head_gain[None], norm_gain[None], expert_ids[0].T, gate_probs[0].T,
        w_gate, w_up, w_down.reshape(L * FF, D),
    )
    return out[None]


def solution(mesh):
    rows = P("exp", "seq", None)
    experts = P("exp", None, None)
    in_specs = (rows, rows, rows, rows, P(), P(), rows, rows, experts, experts, experts)
    return jax.shard_map(
        functools.partial(on_device, mesh.shape["seq"], mesh.shape["exp"]),
        mesh=mesh, in_specs=in_specs, out_specs=rows, check_vma=False,
    )
```
